32 devices in a mesh: rows: 16 (over z, y, core), maps: 2 (over x).
Axes of the slice: x: 2, y: 2, z: 4, core: 2. Of those that a mesh axis runs over, the one named last changes fastest.
Arguments:
- counts: int32 [8, 256, 32768], P(None, 'rows', 'maps'), may hold values from 0 to 2999, as said below
- weights: float32 [8], replicated, may hold values from 0.2 to 5
Outputs:
- barycenter: float32 [256, 32768], P('rows', 'maps')
The draws below stay inside these ranges and needn't reach their ends.
Inputs may be any that keep to these rules, and one draw needn't show every extreme that they name: `counts`: each count is drawn evenly below a ceiling that grows with the row from 1000 (first row) to 3000 (last row), times a level of 1 to 4 over 4 that is drawn for each run of 64 columns; the largest count, 2999, is reached in every draw.
All inputs are finite; a program needn't handle non-finite values.
Results may differ from the reference program's by a relative error of at most 0.0001.
Values sent between devices are 32-bit elements; how exact they have to be, the bound alone decides.
A program may use at most 128 MiB of HBM per device.

```python
import math
import jax
import jax.numpy as jnp
from jax import lax

MAPS = 8
WIDTH = 32768
HALF = 8
ITERS = 2
HEIGHT = 256


def draw_counts(key, part):
    level_key = jax.random.fold_in(key, 17)
    point_key = jax.random.fold_in(key, 29)
    row_index = lax.broadcasted_iota(jnp.int32, (MAPS, HEIGHT, WIDTH), 1)
    ceiling = 1000 + 2000 * row_index // (HEIGHT - 1)
    levels = jax.random.randint(level_key, (MAPS, HEIGHT, WIDTH // 64), 1, 5)
    levels = jnp.repeat(levels, 64, axis=2)
    upper = ceiling * levels // 4
    raw_counts = jax.random.randint(point_key, (MAPS, HEIGHT, WIDTH), 0, upper)
    return raw_counts.at[0, HEIGHT - 1, 0].set(2999).astype(jnp.int32)


def setup_inputs(seed: int = 0) -> dict:
    splits = jax.random.split(jax.random.key(seed), 3)
    counts = draw_counts(jax.random.fold_in(splits[2], 71), 0)
    weights = jnp.clip(jnp.exp(jax.random.uniform(splits[1], (MAPS,), jnp.float32, math.log(0.2), math.log(5.0))), 0.2, 5.0)
    return dict(counts=counts, weights=weights)


def kernel_vector():
    spread = 0.45 * HALF
    across = jnp.arange(-HALF, HALF + 1).astype(jnp.float32)
    shape_taps = jnp.exp(-across * across / (2.0 * spread * spread))
    return shape_taps / jnp.sum(shape_taps)


def smooth_axis(grid_field, kernel_taps, direction):
    padding = [(0, 0), (0, 0)]
    padding[direction] = (HALF, HALF)
    padded = jnp.pad(grid_field, padding)
    length = grid_field.shape[direction]
    result = jnp.zeros(grid_field.shape, jnp.float32)
    for offset in range(2 * HALF + 1):
        result = result + kernel_taps[offset] * lax.slice_in_dim(padded, offset, offset + length, axis=direction)
    return result


def smooth_map(grid_field):
    kernel_taps = kernel_vector()
    return smooth_axis(smooth_axis(grid_field, kernel_taps, 0), kernel_taps, 1)


def reference(counts, weights):
    smoothed = counts.astype(jnp.float32) + 1.0
    totals = jnp.sum(smoothed, axis=(1, 2))
    cell_count = float(HEIGHT * WIDTH)
    density = smoothed * (cell_count / totals)[:, None, None]
    mixing = weights / jnp.sum(weights)
    scaling = jnp.ones(density.shape, jnp.float32)
    barycenter = jnp.zeros((HEIGHT, WIDTH), jnp.float32)
    for iteration in range(ITERS):
        forward = lax.map(smooth_map, scaling)
        dual_scale = density / forward
        marginal = scaling * lax.map(smooth_map, dual_scale)
        barycenter = jnp.exp(jnp.sum(mixing[:, None, None] * jnp.log(marginal), axis=0))
        if iteration + 1 < ITERS:
            scaling = scaling * barycenter[None] / marginal
    return barycenter
```

```python
import functools

import jax
import jax.numpy as jnp
import ml_dtypes
import numpy as np
from jax import lax
from jax.experimental import pallas as pl
from jax.experimental.pallas import tpu as pltpu
from jax.sharding import PartitionSpec as P

HALF = 8
GROUP = 4
EDGE = 128
CHUNK = 256
LAG = 1
MESH = pl.DeviceIdType.MESH


def taps():
    across = np.arange(-HALF, HALF + 1).astype(np.float32)
    spread = 0.45 * HALF
    shape_taps = np.exp(-across * across / np.float32(2.0 * spread * spread))
    return (shape_taps / shape_taps.sum()).astype(np.float32)


def tap_table(offset):
    table = np.zeros(offset.shape, np.float32)
    inside = np.abs(offset) <= HALF
    table[inside] = taps()[offset[inside] + HALF]
    return table


def split(table):
    high = table.astype(ml_dtypes.bfloat16)
    return high, (table - high.astype(np.float32)).astype(ml_dtypes.bfloat16)


def column_table():
    out_col = np.arange(CHUNK)[None, :]
    in_col = np.concatenate(
        [np.arange(CHUNK), np.arange(-EDGE, 0), np.arange(CHUNK, CHUNK + EDGE)]
    )[:, None]
    high, low = split(tap_table(in_col - out_col))
    return np.concatenate([high, high, low], axis=0)


def row_table(rows):
    padded = rows + 2 * HALF
    offset = np.arange(padded)[None, :] - HALF - np.arange(rows)[:, None]
    high, low = split(tap_table(offset))
    fill = -3 * padded % 256
    return np.concatenate([high, high, low, np.zeros((rows, fill), high.dtype)], axis=1)


def window_factor(position, length):
    g = taps()
    total = jnp.zeros(position.shape, jnp.float32)
    for a in range(-HALF, HALF + 1):
        there = (position + a >= 0) & (position + a < length)
        total = total + jnp.where(there, float(g[a + HALF]), 0.0)
    inside = (position >= 0) & (position < length)
    return jnp.where(inside, 1.0 / jnp.where(inside, total, 1.0), 0.0)


def kernel(
    height, width, counts, mix, col_table, row_tab, out,
    cnt, scal, dual, obuf, row_fac, col_fac,
    csend, crecv, esend, erecv, xsend, hsend, hrecv, osend, orecv,
):
    maps, band, tile = counts.shape
    own = tile // GROUP
    cols = own + 2 * EDGE
    chunks = cols // CHUNK
    rows = GROUP * band
    padded = rows + 2 * HALF
    r, x = lax.axis_index("rows"), lax.axis_index("maps")
    groups, x_count = lax.axis_size("rows") // GROUP, lax.axis_size("maps")
    q, p = r // GROUP, r % GROUP

    def peer(k):
        return lax.rem(p + k, GROUP)

    barrier = pltpu.get_barrier_semaphore()

    def greet(row, col):
        pl.semaphore_signal(barrier, inc=1, device_id=(row, col), device_id_type=MESH)

    for k in range(1, GROUP):
        greet(q * GROUP + peer(k), x)
    for there, row in ((q > 0, r - GROUP), (q < groups - 1, r + GROUP)):
        @pl.when(there)
        def _():
            greet(row, x)
    for there, col in ((x > 0, x - 1), (x < x_count - 1, x + 1)):
        @pl.when(there)
        def _():
            for b in range(GROUP):
                greet(q * GROUP + b, col)
    up, down = (q > 0).astype(jnp.int32), (q < groups - 1).astype(jnp.int32)
    left, right = (x > 0).astype(jnp.int32), (x < x_count - 1).astype(jnp.int32)
    pl.semaphore_wait(barrier, GROUP - 1 + up + down + GROUP * (left + right))

    def aligned(value, to):
        return pl.multiple_of(value, to)

    def band_rows(b):
        return pl.ds(aligned(HALF + band * b, HALF), band)

    def piece(source_col, target_col, size, b):
        src = counts.at[:, :, pl.ds(aligned(source_col, EDGE), size)]
        dst = cnt.at[:, band_rows(b), pl.ds(aligned(target_col, EDGE), size)]
        return src, dst

    def count_copy(k, source_col, target_col, size, b, send, recv):
        src, dst = piece(source_col, target_col, size, b)
        if k == 0:
            return pltpu.make_async_copy(src, dst, recv)
        return pltpu.make_async_remote_copy(
            src_ref=src, dst_ref=dst, send_sem=send, recv_sem=recv,
            device_id=(q * GROUP + peer(k), x), device_id_type=MESH,
        )

    def main_copy(k, j, target, b, where):
        send, recv = csend.at[j, k], crecv.at[j, b]
        start = target * own
        if where == 0:
            return count_copy(k, start, EDGE, EDGE, b, send, recv)
        if where == 1:
            return count_copy(
                k, start - EDGE + CHUNK * j, CHUNK * j, CHUNK, b, send, recv)
        return count_copy(k, start + own - EDGE, cols - 2 * EDGE, EDGE, b, send, recv)

    def edge_copy(k, side, target, b):
        source = target * own + (own if side else -EDGE)
        return count_copy(
            k, source, (cols - EDGE) if side else 0, EDGE, b,
            esend.at[side, k], erecv.at[side, b])

    def x_copy(side, target_x, b):
        src, dst = piece(0 if side else tile - EDGE, (cols - EDGE) if side else 0, EDGE, b)
        return pltpu.make_async_remote_copy(
            src_ref=src, dst_ref=dst, send_sem=xsend.at[side], recv_sem=erecv.at[side, b],
            device_id=(q * GROUP + (GROUP - 1 if side else 0), target_x),
            device_id_type=MESH,
        )

    def has_edge(target, side):
        return (target < GROUP - 1) if side else (target > 0)

    def send_edges(side):
        for k in (1, 2, 3, 0):
            @pl.when(has_edge(peer(k), side))
            def _():
                edge_copy(k, side, peer(k), p).start()
        @pl.when((x > 0) if side else (x < x_count - 1))
        def _():
            x_copy(side, x - 1 if side else x + 1, p).start()

    for k in (1, 2, 3, 0):
        main_copy(k, 0, peer(k), p, 0).start()
    send_edges(0)

    @pl.loop(1, chunks - 1)
    def _(j):
        for k in (1, 2, 3, 0):
            main_copy(k, j, peer(k), p, 1).start()

    for k in (1, 2, 3, 0):
        main_copy(k, chunks - 1, peer(k), p, 2).start()
    send_edges(1)

    row_pos = q * rows - HALF + lax.broadcasted_iota(jnp.int32, row_fac.shape, 0)
    row_fac[...] = window_factor(row_pos, height)
    col_pos = x * tile + p * own - EDGE + lax.broadcasted_iota(jnp.int32, col_fac.shape, 1)
    col_fac[...] = window_factor(col_pos, width)
    for there, first in ((q == 0, 0), (q == groups - 1, HALF + rows)):
        @pl.when(there)
        def _():
            for buf in (cnt, scal, dual):
                @pl.loop(0, maps)
                def _(m):
                    buf[m, first:first + HALF, :] = jnp.zeros((HALF, cols), buf.dtype)
    for there, first in (
        ((x == 0) & (p == 0), 0),
        ((x == x_count - 1) & (p == GROUP - 1), cols - EDGE),
    ):
        @pl.when(there)
        def _():
            for m in range(maps):
                cnt[m, HALF:HALF + rows, first:first + EDGE] = jnp.zeros((rows, EDGE), jnp.int32)

    def wait_edges(side):
        inner = has_edge(p, side)
        outer = jnp.logical_not(inner) & ((x < x_count - 1) if side else (x > 0))
        @pl.when(inner)
        def _():
            for k in range(GROUP):
                copy = edge_copy(k, side, p, peer(k))
                copy.wait() if k == 0 else copy.wait_recv()
        @pl.when(outer)
        def _():
            for b in range(GROUP):
                x_copy(side, x + 1 if side else x - 1, b).wait_recv()

    def wait_counts(j):
        def wait(where):
            for k in range(GROUP):
                copy = main_copy(k, j, p, peer(k), where)
                copy.wait() if k == 0 else copy.wait_recv()
        @pl.when(j == 0)
        def _():
            wait(0)
            wait_edges(0)
        @pl.when((j > 0) & (j < chunks - 1))
        def _():
            wait(1)
        @pl.when(j == chunks - 1)
        def _():
            wait(2)
            wait_edges(1)

    def halo_copy(stage, j, way):
        buf = (cnt, scal, dual)[stage]
        source, target = ((rows, 0) if way else (HALF, HALF + rows))
        lanes = pl.ds(aligned(CHUNK * j, CHUNK), CHUNK)
        return pltpu.make_async_remote_copy(
            src_ref=buf.at[:, pl.ds(source, HALF), lanes],
            dst_ref=buf.at[:, pl.ds(target, HALF), lanes],
            send_sem=hsend.at[stage, j, way], recv_sem=hrecv.at[stage, j, way],
            device_id=(r + GROUP if way else r - GROUP, x), device_id_type=MESH,
        )

    def send_halo(stage, j):
        @pl.when(q > 0)
        def _():
            halo_copy(stage, j, 0).start()
        @pl.when(q < groups - 1)
        def _():
            halo_copy(stage, j, 1).start()

    def wait_halo(stage, j):
        @pl.when((j >= 0) & (j < chunks))
        def _():
            @pl.when(q < groups - 1)
            def _():
                halo_copy(stage, j, 0).wait_recv()
            @pl.when(q > 0)
            def _():
                halo_copy(stage, j, 1).wait_recv()

    def halves(value):
        high = value.astype(jnp.bfloat16)
        return high, (value - high.astype(jnp.float32)).astype(jnp.bfloat16)

    def smooth(load, start):
        before = jnp.maximum(start - EDGE, 0)
        after = jnp.minimum(start + CHUNK, cols - EDGE)
        parts = [halves(load(aligned(s, EDGE))) for s in (start, start + EDGE, before, after)]
        high, low = [a for a, _ in parts], [b for _, b in parts]
        lhs = jnp.concatenate(high + low + high, axis=-1).reshape(maps * padded, 6 * CHUNK)
        across = jnp.dot(lhs, col_table[...], preferred_element_type=jnp.float32)
        high, low = halves(across.reshape(maps, padded, CHUNK))
        fill = jnp.zeros((row_tab.shape[1] - 3 * padded, CHUNK), jnp.bfloat16)
        return [
            jnp.dot(
                row_tab[...],
                jnp.concatenate([high[m], low[m], high[m], fill], axis=0),
                preferred_element_type=jnp.float32,
            )
            for m in range(maps)
        ]

    def load_first(s):
        factor = row_fac[...] * col_fac[0:1, pl.ds(s, EDGE)]
        return (cnt[:, :, pl.ds(s, EDGE)].astype(jnp.float32) + 1.0) * factor[None]

    def load_scal(s):
        return scal[:, :, pl.ds(s, EDGE)]

    def load_dual(s):
        return dual[:, :, pl.ds(s, EDGE)]

    def mean_log(logs):
        total = mix[0] * logs[0]
        for m in range(1, maps):
            total = total + mix[m] * logs[m]
        return total

    def stage_a(j):
        start = aligned(CHUNK * j, CHUNK)
        lanes = pl.ds(start, CHUNK)
        logs = [jnp.log(value) for value in smooth(load_first, start)]
        mean = mean_log(logs)
        inside = jnp.broadcast_to(col_fac[0:1, lanes], (rows, CHUNK)) > 0.0
        for m in range(maps):
            scal[m, HALF:HALF + rows, lanes] = jnp.where(inside, jnp.exp(mean - logs[m]), 0.0)

    def stage_b(j):
        start = aligned(CHUNK * j, CHUNK)
        lanes = pl.ds(start, CHUNK)
        forward = smooth(load_scal, start)
        inside = jnp.broadcast_to(col_fac[0:1, lanes], (rows, CHUNK)) > 0.0
        for m in range(maps):
            points = cnt[m, HALF:HALF + rows, lanes].astype(jnp.float32) + 1.0
            dual[m, HALF:HALF + rows, lanes] = jnp.where(inside, points / forward[m], 0.0)

    def out_copy(k, j, target, source):
        src = obuf.at[pl.ds(aligned(band * target, HALF), band),
                      pl.ds(aligned(CHUNK * j, CHUNK), CHUNK)]
        dst = out.at[:, pl.ds(aligned(own * source + CHUNK * j, CHUNK), CHUNK)]
        if k == 0:
            return pltpu.make_async_copy(src, dst, orecv.at[j, source])
        return pltpu.make_async_remote_copy(
            src_ref=src, dst_ref=dst, send_sem=osend.at[j, k], recv_sem=orecv.at[j, source],
            device_id=(q * GROUP + peer(k), x), device_id_type=MESH,
        )

    def stage_c(j):
        start = aligned(EDGE + CHUNK * j, EDGE)
        mean = mean_log([jnp.log(value) for value in smooth(load_dual, start)])
        obuf[:, pl.ds(aligned(CHUNK * j, CHUNK), CHUNK)] = jnp.exp(mean)
        for k in (1, 2, 3, 0):
            out_copy(k, j, peer(k), p).start()

    @pl.loop(0, chunks + 3 * LAG + 2)
    def _(t):
        @pl.when(t < chunks)
        def _():
            wait_counts(t)
            send_halo(0, t)

        a = t - LAG - 1
        wait_halo(0, a + 1)
        @pl.when((a >= 0) & (a < chunks))
        def _():
            stage_a(a)
            send_halo(1, a)

        b = a - LAG - 1
        wait_halo(1, b + 1)
        @pl.when((b >= 0) & (b < chunks))
        def _():
            stage_b(b)
            send_halo(2, b)

        c = b - LAG - 1
        wait_halo(2, c + 1)
        @pl.when((c >= 0) & (c < chunks - 1))
        def _():
            stage_c(c)

    for k in range(1, GROUP):
        main_copy(k, 0, peer(k), p, 0).wait_send()
        main_copy(k, chunks - 1, peer(k), p, 2).wait_send()
        for side in range(2):
            @pl.when(has_edge(peer(k), side))
            def _():
                edge_copy(k, side, peer(k), p).wait_send()
    for side in range(2):
        @pl.when((x > 0) if side else (x < x_count - 1))
        def _():
            x_copy(side, x - 1 if side else x + 1, p).wait_send()

    @pl.loop(1, chunks - 1)
    def _(j):
        for k in range(1, GROUP):
            main_copy(k, j, peer(k), p, 1).wait_send()

    @pl.loop(0, chunks)
    def _(j):
        for stage in range(3):
            @pl.when(q > 0)
            def _():
                halo_copy(stage, j, 0).wait_send()
            @pl.when(q < groups - 1)
            def _():
                halo_copy(stage, j, 1).wait_send()

    @pl.loop(0, chunks - 1)
    def _(j):
        out_copy(0, j, p, p).wait()
        for k in range(1, GROUP):
            out_copy(k, j, peer(k), p).wait_send()
            out_copy(k, j, p, peer(k)).wait_recv()


def on_device(counts, weights):
    maps, band, tile = counts.shape
    height, width = lax.axis_size("rows") * band, lax.axis_size("maps") * tile
    own = tile // GROUP
    cols = own + 2 * EDGE
    chunks = cols // CHUNK
    rows = GROUP * band
    padded = rows + 2 * HALF

    points = jnp.sum(counts + 1, axis=(1, 2)).astype(jnp.float32)
    totals = lax.psum(points, ("rows", "maps"))
    mixing = weights / jnp.sum(weights)

    col_table, row_tab = column_table(), row_table(rows)
    dma = pltpu.SemaphoreType.DMA
    vmem = pl.BlockSpec(memory_space=pltpu.VMEM)
    result = pl.pallas_call(
        functools.partial(kernel, height, width),
        out_shape=jax.ShapeDtypeStruct((band, tile), jnp.float32),
        in_specs=[
            pl.BlockSpec(memory_space=pl.ANY),
            pl.BlockSpec(memory_space=pltpu.SMEM),
            vmem,
            vmem,
        ],
        out_specs=pl.BlockSpec(memory_space=pl.ANY),
        scratch_shapes=[
            pltpu.VMEM((maps, padded, cols), jnp.int32),
            pltpu.VMEM((maps, padded, cols), jnp.float32),
            pltpu.VMEM((maps, padded, cols), jnp.float32),
            pltpu.VMEM((rows, own), jnp.float32),
            pltpu.VMEM((padded, EDGE), jnp.float32),
            pltpu.VMEM((8, cols), jnp.float32),
            dma((chunks, GROUP)),
            dma((chunks, GROUP)),
            dma((2, GROUP)),
            dma((2, GROUP)),
            dma((2,)),
            dma((3, chunks, 2)),
            dma((3, chunks, 2)),
            dma((chunks, GROUP)),
            dma((chunks, GROUP)),
        ],
        compiler_params=pltpu.CompilerParams(
            collective_id=0, has_side_effects=True, vmem_limit_bytes=56 * 1024 * 1024
        ),
        cost_estimate=pl.CostEstimate(
            flops=10**11, bytes_accessed=10**8, transcendentals=10**7
        ),
    )(counts, mixing, jnp.asarray(col_table), jnp.asarray(row_tab))

    scales = float(height * width) / totals
    return result * jnp.exp(jnp.sum(mixing * jnp.log(scales)))


def solution(mesh):
    in_specs = (P(None, "rows", "maps"), P())
    out_specs = P("rows", "maps")
    return jax.shard_map(
        on_device, mesh=mesh, in_specs=in_specs, out_specs=out_specs, check_vma=False
    )
```

```python
import functools

import jax
import jax.numpy as jnp
import ml_dtypes
import numpy as np
from jax import lax
from jax.experimental import pallas as pl
from jax.experimental.pallas import tpu as pltpu
from jax.sharding import PartitionSpec as P

HALF = 8
GROUP = 4
EDGE = 128
CHUNK = 256
LAG = 1
MESH = pl.DeviceIdType.MESH


def taps():
    across = np.arange(-HALF, HALF + 1).astype(np.float32)
    spread = 0.45 * HALF
    shape_taps = np.exp(-across * across / np.float32(2.0 * spread * spread))
    return (shape_taps / shape_taps.sum()).astype(np.float32)


def tap_table(offset):
    table = np.zeros(offset.shape, np.float32)
    inside = np.abs(offset) <= HALF
    table[inside] = taps()[offset[inside] + HALF]
    return table


def split(table):
    high = table.astype(ml_dtypes.bfloat16)
    return high, (table - high.astype(np.float32)).astype(ml_dtypes.bfloat16)


def column_table():
    out_col = np.arange(CHUNK)[None, :]
    in_col = np.concatenate(
        [np.arange(CHUNK), np.arange(-EDGE, 0), np.arange(CHUNK, CHUNK + EDGE)]
    )[:, None]
    high, low = split(tap_table(in_col - out_col))
    return np.concatenate([high, high, low], axis=0)


def row_table(rows):
    padded = rows + 2 * HALF
    offset = np.arange(padded)[None, :] - HALF - np.arange(rows)[:, None]
    high, low = split(tap_table(offset))
    fill = -3 * padded % 256
    return np.concatenate([high, high, low, np.zeros((rows, fill), high.dtype)], axis=1)


def window_factor(position, length):
    g = taps()
    total = jnp.zeros(position.shape, jnp.float32)
    for a in range(-HALF, HALF + 1):
        there = (position + a >= 0) & (position + a < length)
        total = total + jnp.where(there, float(g[a + HALF]), 0.0)
    inside = (position >= 0) & (position < length)
    return jnp.where(inside, 1.0 / jnp.where(inside, total, 1.0), 0.0)


def kernel(
    height, width, counts, weights, col_table, row_tab, out, factor_out,
    cnt, scal, dual, obuf, row_fac, col_fac,
    csend, crecv, esend, erecv, xsend, hsend, hrecv, osend, orecv,
    points, part, running, arrived, psend, precv, tsend, trecv,
):
    maps, band, tile = counts.shape
    own = tile // GROUP
    cols = own + 2 * EDGE
    chunks = cols // CHUNK
    rows = GROUP * band
    padded = rows + 2 * HALF
    r, x = lax.axis_index("rows"), lax.axis_index("maps")
    groups, x_count = lax.axis_size("rows") // GROUP, lax.axis_size("maps")
    q, p = r // GROUP, r % GROUP

    def peer(k):
        return lax.rem(p + k, GROUP)

    doubling = [(0, 1 << i) for i in range(groups.bit_length() - 1)]
    doubling += [(1, 1 << i) for i in range(x_count.bit_length() - 1)]

    def partner(axis, step):
        place = (q, x)[axis]
        other = place + (1 - 2 * lax.rem(place // step, 2)) * step
        return (other * GROUP + p, x) if axis == 0 else (r, other)

    barrier = pltpu.get_barrier_semaphore()

    def greet(row, col):
        pl.semaphore_signal(barrier, inc=1, device_id=(row, col), device_id_type=MESH)

    for k in range(1, GROUP):
        greet(q * GROUP + peer(k), x)
    for there, row in ((q > 0, r - GROUP), (q < groups - 1, r + GROUP)):
        @pl.when(there)
        def _():
            greet(row, x)
    for there, col in ((x > 0, x - 1), (x < x_count - 1, x + 1)):
        @pl.when(there)
        def _():
            for b in range(GROUP):
                greet(q * GROUP + b, col)
    far = [(axis, step) for axis, step in doubling if step > 1]
    for axis, step in far:
        greet(*partner(axis, step))
    up, down = (q > 0).astype(jnp.int32), (q < groups - 1).astype(jnp.int32)
    left, right = (x > 0).astype(jnp.int32), (x < x_count - 1).astype(jnp.int32)
    pl.semaphore_wait(barrier, GROUP - 1 + len(far) + up + down + GROUP * (left + right))

    def aligned(value, to):
        return pl.multiple_of(value, to)

    def band_rows(b):
        return pl.ds(aligned(HALF + band * b, HALF), band)

    def piece(source_col, target_col, size, b):
        src = counts.at[:, :, pl.ds(aligned(source_col, EDGE), size)]
        dst = cnt.at[:, band_rows(b), pl.ds(aligned(target_col, EDGE), size)]
        return src, dst

    def count_copy(k, source_col, target_col, size, b, send, recv):
        src, dst = piece(source_col, target_col, size, b)
        if k == 0:
            return pltpu.make_async_copy(src, dst, recv)
        return pltpu.make_async_remote_copy(
            src_ref=src, dst_ref=dst, send_sem=send, recv_sem=recv,
            device_id=(q * GROUP + peer(k), x), device_id_type=MESH,
        )

    def main_copy(k, j, target, b, where):
        send, recv = csend.at[j, k], crecv.at[j, b]
        start = target * own
        if where == 0:
            return count_copy(k, start, EDGE, EDGE, b, send, recv)
        if where == 1:
            return count_copy(
                k, start - EDGE + CHUNK * j, CHUNK * j, CHUNK, b, send, recv)
        return count_copy(k, start + own - EDGE, cols - 2 * EDGE, EDGE, b, send, recv)

    def edge_copy(k, side, target, b):
        source = target * own + (own if side else -EDGE)
        return count_copy(
            k, source, (cols - EDGE) if side else 0, EDGE, b,
            esend.at[side, k], erecv.at[side, b])

    def x_copy(side, target_x, b):
        src, dst = piece(0 if side else tile - EDGE, (cols - EDGE) if side else 0, EDGE, b)
        return pltpu.make_async_remote_copy(
            src_ref=src, dst_ref=dst, send_sem=xsend.at[side], recv_sem=erecv.at[side, b],
            device_id=(q * GROUP + (GROUP - 1 if side else 0), target_x),
            device_id_type=MESH,
        )

    def has_edge(target, side):
        return (target < GROUP - 1) if side else (target > 0)

    def send_edges(side):
        for k in (1, 2, 3, 0):
            @pl.when(has_edge(peer(k), side))
            def _():
                edge_copy(k, side, peer(k), p).start()
        @pl.when((x > 0) if side else (x < x_count - 1))
        def _():
            x_copy(side, x - 1 if side else x + 1, p).start()

    for k in (1, 2, 3, 0):
        main_copy(k, 0, peer(k), p, 0).start()
    send_edges(0)

    @pl.loop(1, chunks - 1)
    def _(j):
        for k in (1, 2, 3, 0):
            main_copy(k, j, peer(k), p, 1).start()

    for k in (1, 2, 3, 0):
        main_copy(k, chunks - 1, peer(k), p, 2).start()
    send_edges(1)

    row_pos = q * rows - HALF + lax.broadcasted_iota(jnp.int32, row_fac.shape, 0)
    row_fac[...] = window_factor(row_pos, height)
    col_pos = x * tile + p * own - EDGE + lax.broadcasted_iota(jnp.int32, col_fac.shape, 1)
    col_fac[...] = window_factor(col_pos, width)
    for there, first in ((q == 0, 0), (q == groups - 1, HALF + rows)):
        @pl.when(there)
        def _():
            for buf in (cnt, scal, dual):
                @pl.loop(0, maps)
                def _(m):
                    buf[m, first:first + HALF, :] = jnp.zeros((HALF, cols), buf.dtype)
    for there, first in (
        ((x == 0) & (p == 0), 0),
        ((x == x_count - 1) & (p == GROUP - 1), cols - EDGE),
    ):
        @pl.when(there)
        def _():
            for m in range(maps):
                cnt[m, HALF:HALF + rows, first:first + EDGE] = jnp.zeros((rows, EDGE), jnp.int32)

    def wait_edges(side):
        inner = has_edge(p, side)
        outer = jnp.logical_not(inner) & ((x < x_count - 1) if side else (x > 0))
        @pl.when(inner)
        def _():
            for k in range(GROUP):
                copy = edge_copy(k, side, p, peer(k))
                copy.wait() if k == 0 else copy.wait_recv()
        @pl.when(outer)
        def _():
            for b in range(GROUP):
                x_copy(side, x + 1 if side else x - 1, b).wait_recv()

    def wait_counts(j):
        def wait(where):
            for k in range(GROUP):
                copy = main_copy(k, j, p, peer(k), where)
                copy.wait() if k == 0 else copy.wait_recv()
        @pl.when(j == 0)
        def _():
            wait(0)
            wait_edges(0)
        @pl.when((j > 0) & (j < chunks - 1))
        def _():
            wait(1)
        @pl.when(j == chunks - 1)
        def _():
            wait(2)
            wait_edges(1)

    def halo_copy(stage, j, way):
        buf = (cnt, scal, dual)[stage]
        source, target = ((rows, 0) if way else (HALF, HALF + rows))
        lanes = pl.ds(aligned(CHUNK * j, CHUNK), CHUNK)
        return pltpu.make_async_remote_copy(
            src_ref=buf.at[:, pl.ds(source, HALF), lanes],
            dst_ref=buf.at[:, pl.ds(target, HALF), lanes],
            send_sem=hsend.at[stage, j, way], recv_sem=hrecv.at[stage, j, way],
            device_id=(r + GROUP if way else r - GROUP, x), device_id_type=MESH,
        )

    def send_halo(stage, j):
        @pl.when(q > 0)
        def _():
            halo_copy(stage, j, 0).start()
        @pl.when(q < groups - 1)
        def _():
            halo_copy(stage, j, 1).start()

    def wait_halo(stage, j):
        @pl.when((j >= 0) & (j < chunks))
        def _():
            @pl.when(q < groups - 1)
            def _():
                halo_copy(stage, j, 0).wait_recv()
            @pl.when(q > 0)
            def _():
                halo_copy(stage, j, 1).wait_recv()

    def halves(value):
        high = value.astype(jnp.bfloat16)
        return high, (value - high.astype(jnp.float32)).astype(jnp.bfloat16)

    def smooth(load, start):
        before = jnp.maximum(start - EDGE, 0)
        after = jnp.minimum(start + CHUNK, cols - EDGE)
        parts = [halves(load(aligned(s, EDGE))) for s in (start, start + EDGE, before, after)]
        high, low = [a for a, _ in parts], [b for _, b in parts]
        lhs = jnp.concatenate(high + low + high, axis=-1).reshape(maps * padded, 6 * CHUNK)
        across = jnp.dot(lhs, col_table[...], preferred_element_type=jnp.float32)
        high, low = halves(across.reshape(maps, padded, CHUNK))
        fill = jnp.zeros((row_tab.shape[1] - 3 * padded, CHUNK), jnp.bfloat16)
        return [
            jnp.dot(
                row_tab[...],
                jnp.concatenate([high[m], low[m], high[m], fill], axis=0),
                preferred_element_type=jnp.float32,
            )
            for m in range(maps)
        ]

    def load_first(s):
        factor = row_fac[...] * col_fac[0:1, pl.ds(s, EDGE)]
        return (cnt[:, :, pl.ds(s, EDGE)].astype(jnp.float32) + 1.0) * factor[None]

    def load_scal(s):
        return scal[:, :, pl.ds(s, EDGE)]

    def load_dual(s):
        return dual[:, :, pl.ds(s, EDGE)]

    weight_sum = weights[0]
    for m in range(1, maps):
        weight_sum = weight_sum + weights[m]

    def mean_log(logs):
        total = weights[0] * logs[0]
        for m in range(1, maps):
            total = total + weights[m] * logs[m]
        return total * (1.0 / jnp.full((1, CHUNK), weight_sum, jnp.float32))

    points[...] = jnp.zeros(points.shape, jnp.int32)

    def add_points(j):
        start = aligned(EDGE + CHUNK * j, EDGE)
        for m in range(maps):
            block = cnt[m, HALF:HALF + rows, pl.ds(start, CHUNK)] + 1
            block = block[:, :EDGE] + block[:, EDGE:]
            points[m] += jnp.sum(block.reshape(rows // 8, 8, EDGE), axis=0)

    def part_copy(k, source):
        return pltpu.make_async_remote_copy(
            src_ref=part.at[source], dst_ref=part.at[source],
            send_sem=psend.at[k], recv_sem=precv.at[source],
            device_id=(q * GROUP + peer(k), x), device_id_type=MESH,
        )

    def doubling_copy(i):
        return pltpu.make_async_remote_copy(
            src_ref=running.at[i], dst_ref=arrived.at[i],
            send_sem=tsend.at[i], recv_sem=trecv.at[i],
            device_id=partner(*doubling[i]), device_id_type=MESH,
        )

    def totals_step(i):
        if i == 0:
            sums = jnp.concatenate(
                [jnp.sum(points[m], axis=0, keepdims=True) for m in range(maps)], axis=0)
            sums = jnp.sum(sums, axis=1, keepdims=True).astype(jnp.float32)
            part[p] = jnp.broadcast_to(sums, (maps, EDGE))
            for k in range(1, GROUP):
                part_copy(k, p).start()
            return
        if i == 1:
            for k in range(1, GROUP):
                part_copy(k, peer(k)).wait_recv()
            total = part[0]
            for b in range(1, GROUP):
                total = total + part[b]
        else:
            doubling_copy(i - 2).wait_recv()
            total = running[i - 2] + arrived[i - 2]
        if i <= len(doubling):
            running[i - 1] = total
            doubling_copy(i - 1).start()
            return
        which = lax.broadcasted_iota(jnp.int32, total.shape, 0)
        mixing = jnp.zeros(total.shape, jnp.float32)
        for m in range(maps):
            mixing = jnp.where(which == m, weights[m], mixing)
        mixing = mixing / jnp.full(total.shape, weight_sum, jnp.float32)
        mean = jnp.sum(mixing * jnp.log(float(height * width) / total), axis=0, keepdims=True)
        factor_out[...] = jnp.broadcast_to(jnp.exp(mean), factor_out.shape)

    def stage_a(j):
        start = aligned(CHUNK * j, CHUNK)
        lanes = pl.ds(start, CHUNK)
        logs = [jnp.log(value) for value in smooth(load_first, start)]
        mean = mean_log(logs)
        inside = jnp.broadcast_to(col_fac[0:1, lanes], (rows, CHUNK)) > 0.0
        for m in range(maps):
            scal[m, HALF:HALF + rows, lanes] = jnp.where(inside, jnp.exp(mean - logs[m]), 0.0)

    def stage_b(j):
        start = aligned(CHUNK * j, CHUNK)
        lanes = pl.ds(start, CHUNK)
        forward = smooth(load_scal, start)
        inside = jnp.broadcast_to(col_fac[0:1, lanes], (rows, CHUNK)) > 0.0
        for m in range(maps):
            points = cnt[m, HALF:HALF + rows, lanes].astype(jnp.float32) + 1.0
            dual[m, HALF:HALF + rows, lanes] = jnp.where(inside, points / forward[m], 0.0)

    def out_copy(k, j, target, source):
        src = obuf.at[pl.ds(aligned(band * target, HALF), band),
                      pl.ds(aligned(CHUNK * j, CHUNK), CHUNK)]
        dst = out.at[:, pl.ds(aligned(own * source + CHUNK * j, CHUNK), CHUNK)]
        if k == 0:
            return pltpu.make_async_copy(src, dst, orecv.at[j, source])
        return pltpu.make_async_remote_copy(
            src_ref=src, dst_ref=dst, send_sem=osend.at[j, k], recv_sem=orecv.at[j, source],
            device_id=(q * GROUP + peer(k), x), device_id_type=MESH,
        )

    def stage_c(j):
        start = aligned(EDGE + CHUNK * j, EDGE)
        mean = mean_log([jnp.log(value) for value in smooth(load_dual, start)])
        obuf[:, pl.ds(aligned(CHUNK * j, CHUNK), CHUNK)] = jnp.exp(mean)
        for k in (1, 2, 3, 0):
            out_copy(k, j, peer(k), p).start()

    @pl.loop(0, chunks + max(3 * LAG + 2, len(doubling) + 1))
    def _(t):
        @pl.when(t < chunks)
        def _():
            wait_counts(t)
            send_halo(0, t)

        @pl.when((t > 0) & (t < chunks))
        def _():
            add_points(t - 1)
        for i in range(len(doubling) + 2):
            @pl.when(t == chunks - 1 + i)
            def _():
                totals_step(i)

        a = t - LAG - 1
        wait_halo(0, a + 1)
        @pl.when((a >= 0) & (a < chunks))
        def _():
            stage_a(a)
            send_halo(1, a)

        b = a - LAG - 1
        wait_halo(1, b + 1)
        @pl.when((b >= 0) & (b < chunks))
        def _():
            stage_b(b)
            send_halo(2, b)

        c = b - LAG - 1
        wait_halo(2, c + 1)
        @pl.when((c >= 0) & (c < chunks - 1))
        def _():
            stage_c(c)

    for k in range(1, GROUP):
        main_copy(k, 0, peer(k), p, 0).wait_send()
        main_copy(k, chunks - 1, peer(k), p, 2).wait_send()
        for side in range(2):
            @pl.when(has_edge(peer(k), side))
            def _():
                edge_copy(k, side, peer(k), p).wait_send()
    for side in range(2):
        @pl.when((x > 0) if side else (x < x_count - 1))
        def _():
            x_copy(side, x - 1 if side else x + 1, p).wait_send()

    for k in range(1, GROUP):
        part_copy(k, p).wait_send()
    for i in range(len(doubling)):
        doubling_copy(i).wait_send()

    @pl.loop(1, chunks - 1)
    def _(j):
        for k in range(1, GROUP):
            main_copy(k, j, peer(k), p, 1).wait_send()

    @pl.loop(0, chunks)
    def _(j):
        for stage in range(3):
            @pl.when(q > 0)
            def _():
                halo_copy(stage, j, 0).wait_send()
            @pl.when(q < groups - 1)
            def _():
                halo_copy(stage, j, 1).wait_send()

    @pl.loop(0, chunks - 1)
    def _(j):
        out_copy(0, j, p, p).wait()
        for k in range(1, GROUP):
            out_copy(k, j, peer(k), p).wait_send()
            out_copy(k, j, p, peer(k)).wait_recv()


def on_device(counts, weights):
    maps, band, tile = counts.shape
    height, width = lax.axis_size("rows") * band, lax.axis_size("maps") * tile
    own = tile // GROUP
    cols = own + 2 * EDGE
    chunks = cols // CHUNK
    rows = GROUP * band
    padded = rows + 2 * HALF

    groups, x_count = lax.axis_size("rows") // GROUP, lax.axis_size("maps")
    rounds = groups.bit_length() + x_count.bit_length() - 2

    col_table, row_tab = column_table(), row_table(rows)
    dma = pltpu.SemaphoreType.DMA
    vmem = pl.BlockSpec(memory_space=pltpu.VMEM)
    result, factor = pl.pallas_call(
        functools.partial(kernel, height, width),
        out_shape=(
            jax.ShapeDtypeStruct((band, tile), jnp.float32),
            jax.ShapeDtypeStruct((maps, EDGE), jnp.float32),
        ),
        in_specs=[
            pl.BlockSpec(memory_space=pl.ANY),
            pl.BlockSpec(memory_space=pltpu.SMEM),
            vmem,
            vmem,
        ],
        out_specs=(pl.BlockSpec(memory_space=pl.ANY), vmem),
        scratch_shapes=[
            pltpu.VMEM((maps, padded, cols), jnp.int32),
            pltpu.VMEM((maps, padded, cols), jnp.float32),
            pltpu.VMEM((maps, padded, cols), jnp.float32),
            pltpu.VMEM((rows, own), jnp.float32),
            pltpu.VMEM((padded, EDGE), jnp.float32),
            pltpu.VMEM((8, cols), jnp.float32),
            dma((chunks, GROUP)),
            dma((chunks, GROUP)),
            dma((2, GROUP)),
            dma((2, GROUP)),
            dma((2,)),
            dma((3, chunks, 2)),
            dma((3, chunks, 2)),
            dma((chunks, GROUP)),
            dma((chunks, GROUP)),
            pltpu.VMEM((maps, 8, EDGE), jnp.int32),
            pltpu.VMEM((GROUP, maps, EDGE), jnp.float32),
            pltpu.VMEM((max(rounds, 1), maps, EDGE), jnp.float32),
            pltpu.VMEM((max(rounds, 1), maps, EDGE), jnp.float32),
            dma((GROUP,)),
            dma((GROUP,)),
            dma((max(rounds, 1),)),
            dma((max(rounds, 1),)),
        ],
        compiler_params=pltpu.CompilerParams(
            collective_id=0, has_side_effects=True, vmem_limit_bytes=56 * 1024 * 1024
        ),
        cost_estimate=pl.CostEstimate(
            flops=10**11, bytes_accessed=10**8, transcendentals=10**7
        ),
    )(counts, weights, jnp.asarray(col_table), jnp.asarray(row_tab))

    return result * factor[0, 0]


def solution(mesh):
    in_specs = (P(None, "rows", "maps"), P())
    out_specs = P("rows", "maps")
    return jax.shard_map(
        on_device, mesh=mesh, in_specs=in_specs, out_specs=out_specs, check_vma=False
    )
```
